32 devices in a mesh: gx: 4 (over y, core), gy: 8 (over z, x).
Axes of the slice: x: 2, y: 2, z: 4, core: 2. Of those that a mesh axis runs over, the one named last changes fastest.
Arguments:
- x_block: float32 [16, 32, 64, 128], P(None, 'gx', 'gy'), may hold values from -8 to 8
- old_direction: float32 [16, 32, 64, 128], P(None, 'gx', 'gy'), may hold values from -6 to 6
- conductivity: float32 [32, 64, 128], P('gx', 'gy'), may hold values from 0.5 to 4
- fsai_diagonal: float32 [32, 64, 128], P('gx', 'gy'), may hold values from 0.2 to 0.6
- fsai_lower: float32 [13, 32, 64, 128], P(None, 'gx', 'gy'), may hold values from -0.9 to 0.9
- pattern: int32 [8, 13], replicated, may hold values 0 or 1
- step_size: float32 [16], replicated, may hold values from 0.3 to 1.5
- momentum: float32 [16], replicated, may hold values from 0.2 to 1
Outputs:
- x_next: float32 [16, 32, 64, 128], P(None, 'gx', 'gy')
- direction: float32 [16, 32, 64, 128], P(None, 'gx', 'gy')
- rayleigh: float32 [16, 16], replicated
The draws below stay inside these ranges and needn't reach their ends.
All inputs are finite; a program needn't handle non-finite values.
Results may differ from the reference program's by a relative error of at most 0.00018.
Values sent between devices are 32-bit elements; how exact they have to be, the bound alone decides.
A program may use at most 64 MiB of HBM per device.

```python
import math
import jax
import jax.numpy as jnp
from jax import lax

K = 16
OFFSETS = 13
BLOCKS = 8
NZ = 128
NX = 32
NY = 64
NCELLS = 262144


def draw_x_block(key, part):
    coord_x = jnp.arange(NX, dtype=jnp.float32) / NX
    coord_y = jnp.arange(NY, dtype=jnp.float32) / NY
    base = jax.random.normal(key, (K, NX, NY, NZ), jnp.float32)
    rate = 3.0
    spread = 0.7 * rate ** (0.5 * (coord_x[:, None] + coord_y[None, :]))
    return jnp.clip(base * spread[None, :, :, None], -8.0, 8.0)


def set_ends(drawn, rng, least, top_value):
    longest = drawn.shape.index(max(drawn.shape))
    spots = []
    for shift in (0, 1):
        where = [jax.random.randint(jax.random.fold_in(rng, axis), (), 0, length) for axis, length in enumerate(drawn.shape)]
        where[longest] = (where[longest] + shift) % drawn.shape[longest]
        spots.append(tuple(where))
    return drawn.at[spots[0]].set(least).at[spots[1]].set(top_value)


def block_levels(stream_key, dims, pieces, least, top_value):
    loudness = 1.0
    for dim, shards_of in pieces:
        heights = jax.random.uniform(jax.random.fold_in(jax.random.fold_in(stream_key, 6), dim), (shards_of,), jnp.float32, least / len(pieces), top_value / len(pieces))
        loudness = loudness * jnp.repeat(jnp.exp(heights), dims[dim] // shards_of).reshape((-1,) + (1,) * (len(dims) - 1 - dim))
    return loudness


def centred(own_key, shape, width, most, split=(), kind=jnp.bfloat16):
    loudness = block_levels(own_key, shape, split, -0.22, 0.18) if split else 1.0
    array = jax.random.normal(own_key, shape, jnp.float32) * width * loudness
    return jnp.minimum(jnp.maximum(array, -most), most).astype(kind)


def setup_inputs(seed: int = 0) -> dict:
    streams_of = jax.random.split(jax.random.key(seed), 9)
    return {
        "x_block": draw_x_block(jax.random.fold_in(streams_of[8], 71), 0),
        "old_direction": centred(streams_of[1], (K, NX, NY, NZ), 1.0, 6.0, ((1, 4), (2, 8)), jnp.float32),
        "conductivity": jnp.clip(jnp.exp(math.log(4.0) - 2.0794415 * jax.random.uniform(streams_of[2], (NX, NY, NZ), jnp.float32) ** block_levels(streams_of[2], (NX, NY, NZ), ((0, 4), (1, 8)), -0.2, 0.2)), 0.5, 4.0),
        "fsai_diagonal": jnp.clip(jnp.exp(math.log(0.6) - 1.0986123 * jax.random.uniform(streams_of[3], (NX, NY, NZ), jnp.float32) ** block_levels(streams_of[3], (NX, NY, NZ), ((0, 4), (1, 8)), -0.2, 0.2)), 0.2, 0.6),
        "fsai_lower": centred(streams_of[4], (OFFSETS, NX, NY, NZ), 0.15, 0.9, ((1, 4), (2, 8)), jnp.float32),
        "pattern": set_ends((jax.random.randint(streams_of[5], (BLOCKS, OFFSETS), 0, 3) < 2).astype(jnp.int32), jax.random.fold_in(streams_of[5], 1), 0, 1),
        "step_size": jnp.clip(jnp.exp(jax.random.uniform(streams_of[6], (K,), jnp.float32, math.log(0.3), math.log(1.5))), 0.3, 1.5),
        "momentum": jnp.clip(jnp.exp(jax.random.uniform(streams_of[7], (K,), jnp.float32, math.log(0.2), math.log(1.0))), 0.2, 1.0),
    }


lower_offsets = [(a, b, c) for a in (-1, 0, 1) for b in (-1, 0, 1) for c in (-1, 0, 1) if (a, b, c) < (0, 0, 0)]
face_offsets = [(1, 0, 0), (-1, 0, 0), (0, 1, 0), (0, -1, 0), (0, 0, 1), (0, 0, -1)]

def window(padded, step_x, step_y, step_z, region):
    size_x, size_y, size_z = region
    return padded[..., 1 + step_x:1 + step_x + size_x, 1 + step_y:1 + step_y + size_y, 1 + step_z:1 + step_z + size_z]

def apply_stiffness(padded, kappa_pad, region):
    centre = window(padded, 0, 0, 0, region)
    kappa_here = window(kappa_pad, 0, 0, 0, region)
    summed = jnp.zeros(centre.shape, jnp.float32)
    for step_x, step_y, step_z in face_offsets:
        face = 0.5 * (kappa_here + window(kappa_pad, step_x, step_y, step_z, region))
        summed = summed + face * (centre - window(padded, step_x, step_y, step_z, region))
    return summed

def apply_factor(padded, diag_here, lower_here, region):
    summed = diag_here * window(padded, 0, 0, 0, region)
    for index, (step_x, step_y, step_z) in enumerate(lower_offsets):
        summed = summed + lower_here[index] * window(padded, step_x, step_y, step_z, region)
    return summed

def apply_transpose(padded, diag_pad, lower_pad, region):
    summed = window(diag_pad, 0, 0, 0, region) * window(padded, 0, 0, 0, region)
    for index, (step_x, step_y, step_z) in enumerate(lower_offsets):
        summed = summed + window(lower_pad[index], -step_x, -step_y, -step_z, region) * window(padded, -step_x, -step_y, -step_z, region)
    return summed

def pad_all(field):
    return jnp.pad(field, ((1, 1), (1, 1), (1, 1)))

def reference(x_block, old_direction, conductivity, fsai_diagonal, fsai_lower, pattern, step_size, momentum):
    region = (NX, NY, NZ)
    block_id = jnp.arange(NZ, dtype=jnp.int32) // (NZ // BLOCKS)
    onehot = (block_id[:, None] == jnp.arange(BLOCKS, dtype=jnp.int32)[None, :]).astype(jnp.float32)
    active = jnp.dot(onehot, pattern.astype(jnp.float32), precision=lax.Precision.HIGHEST)
    lower_terms = fsai_lower * jnp.transpose(active)[:, None, None, :]
    kappa_pad = pad_all(conductivity)
    diag_pad = pad_all(fsai_diagonal)
    lower_pad = jnp.pad(lower_terms, ((0, 0), (1, 1), (1, 1), (1, 1)))
    image = lax.map(lambda vector: apply_stiffness(pad_all(vector), kappa_pad, region), x_block)
    scale = 1.0 / NCELLS
    sum_xx = jnp.sum(x_block * x_block, axis=(1, 2, 3))
    sum_xa = jnp.sum(x_block * image, axis=(1, 2, 3))
    quotient = sum_xa * scale / (sum_xx * scale + 1e-06)
    gradient = image - quotient[:, None, None, None] * x_block

    def precondition(vector):
        product = apply_factor(pad_all(vector), fsai_diagonal, lower_terms, region)
        return apply_transpose(pad_all(product), diag_pad, lower_pad, region)
    smoothed = lax.map(precondition, gradient)
    direction = smoothed + momentum[:, None, None, None] * old_direction
    advanced = x_block + step_size[:, None, None, None] * direction
    direction_image = lax.map(lambda vector: apply_stiffness(pad_all(vector), kappa_pad, region), direction)
    advanced_image = image + step_size[:, None, None, None] * direction_image
    identity = jnp.eye(K, dtype=jnp.float32)
    gram = jnp.einsum('kxyz,jxyz->kj', advanced, advanced, precision=lax.Precision.HIGHEST) * scale + 1e-05 * identity
    stiff = jnp.einsum('kxyz,jxyz->kj', advanced, advanced_image, precision=lax.Precision.HIGHEST) * scale
    factor = jnp.linalg.cholesky(gram)
    inverse = jax.scipy.linalg.solve_triangular(factor, identity, lower=True)
    x_next = jnp.einsum('kj,jxyz->kxyz', inverse, advanced, precision=lax.Precision.HIGHEST)
    rayleigh = jnp.dot(jnp.dot(inverse, stiff, precision=lax.Precision.HIGHEST), jnp.transpose(inverse), precision=lax.Precision.HIGHEST)
    return (x_next, direction, rayleigh)
```

```python
import functools

import jax
import jax.numpy as jnp
from jax import lax
from jax.experimental import pallas as pl
from jax.experimental.pallas import tpu as pltpu
from jax.sharding import PartitionSpec as P

MESH = pl.DeviceIdType.MESH
F32 = jnp.float32
BF16 = jnp.bfloat16

lower_offsets = [
    (a, b, c) for a in (-1, 0, 1) for b in (-1, 0, 1) for c in (-1, 0, 1) if (a, b, c) < (0, 0, 0)
]
DIAG = len(lower_offsets)
SIDES = [(1, 0), (-1, 0), (0, 1), (0, -1)]


def split3(value):
    high = value.astype(BF16)
    rest = value - high.astype(F32)
    middle = rest.astype(BF16)
    low = (rest - middle.astype(F32)).astype(BF16)
    return high, middle, low


def kernel(
    nx, ny, scale,
    x_in, old_in, cond_in, diag_in, lower_in, pattern_in, step_in, mom_in,
    next_out, dir_out, ray_out,
    xs, im, gr, pr, pt, adv,
    recv_x, recv_y0, recv_y1, recv_c, halo_x, halo_y,
    k_side, k_stage, coef, lm, lp,
    ab, abh, q_x, q_y, g_x, g_y,
    send_sem, recv_sem, send_x, recv_gx, send_y, recv_gy,
):
    ix, iy = lax.axis_index("gx"), lax.axis_index("gy")
    size_x, size_y = cond_in.shape[0], cond_in.shape[1]
    depth = cond_in.shape[2]
    vectors = xs.shape[2]
    cells = size_x * size_y
    blocks = pattern_in.shape[0]
    zero_col = jnp.zeros((vectors, depth), F32)
    zero_tile = jnp.zeros((size_y, depth), F32)

    def exists(sx, sy):
        found = None
        for ok, step in (
            (ix + 1 < nx, sx > 0), (ix > 0, sx < 0), (iy + 1 < ny, sy > 0), (iy > 0, sy < 0)
        ):
            if step:
                found = ok if found is None else jnp.logical_and(found, ok)
        return found

    def copy_of(item):
        src, dst, sx, sy, slot = item
        return pltpu.make_async_remote_copy(
            src_ref=src, dst_ref=dst, send_sem=send_sem.at[slot], recv_sem=recv_sem.at[slot],
            device_id=(ix + sx, iy + sy), device_id_type=MESH,
        )

    def start(items):
        for item in items:
            @pl.when(exists(item[2], item[3]))
            def _(item=item):
                copy_of(item).start()

    def wait_recv(items):
        for item in items:
            @pl.when(exists(-item[2], -item[3]))
            def _(item=item):
                copy_of(item).wait_recv()

    def wait_send(items):
        for item in items:
            @pl.when(exists(item[2], item[3]))
            def _(item=item):
                copy_of(item).wait_send()

    def group_start(buf, turn, n, me, place, sends, recvs):
        for s in range(1, n):
            peer = lax.rem(me + s, n)
            pltpu.make_async_remote_copy(
                src_ref=buf.at[me], dst_ref=buf.at[me], send_sem=sends.at[turn, s],
                recv_sem=recvs.at[turn, s], device_id=place(peer), device_id_type=MESH,
            ).start()

    def group_wait(buf, turn, n, me, place, sends, recvs):
        for s in range(1, n):
            peer = lax.rem(me + n - s, n)
            pltpu.make_async_remote_copy(
                src_ref=buf.at[peer], dst_ref=buf.at[peer], send_sem=sends.at[turn, s],
                recv_sem=recvs.at[turn, s], device_id=place(peer), device_id_type=MESH,
            ).wait()

    def along_x(peer):
        return (peer, iy)

    def along_y(peer):
        return (ix, peer)

    def reduce_start(buf_x, turn, tile):
        buf_x[ix] = tile
        group_start(buf_x, turn, nx, ix, along_x, send_x, recv_gx)

    def reduce_finish(buf_x, buf_y, turn):
        group_wait(buf_x, turn, nx, ix, along_x, send_x, recv_gx)
        total = buf_x[0]
        for i in range(1, nx):
            total = total + buf_x[i]
        buf_y[iy] = total
        group_start(buf_y, turn, ny, iy, along_y, send_y, recv_gy)
        group_wait(buf_y, turn, ny, iy, along_y, send_y, recv_gy)
        total = buf_y[0]
        for i in range(1, ny):
            total = total + buf_y[i]
        return total

    for buf in (xs, im):
        for y in range(size_y + 2):
            buf[0, y] = zero_col
            buf[size_x + 1, y] = zero_col
        for x in range(1, size_x + 1):
            buf[x, 0] = zero_col
            buf[x, size_y + 1] = zero_col
    for i in range(4):
        k_side[i] = zero_tile
    for i in range(size_y):
        recv_x[i] = zero_col
        halo_x[i] = zero_col
    for i in range(size_x):
        recv_y0[i] = zero_col
        recv_y1[i] = zero_col
        halo_y[i] = zero_col
    recv_c[0] = zero_col
    recv_c[1] = zero_col

    barrier = pltpu.get_barrier_semaphore()
    for s in range(1, nx):
        pl.semaphore_signal(barrier, inc=1, device_id=along_x(lax.rem(ix + s, nx)), device_id_type=MESH)
    for s in range(1, ny):
        pl.semaphore_signal(barrier, inc=1, device_id=along_y(lax.rem(iy + s, ny)), device_id_type=MESH)
    diagonal = 0
    for sx in (-1, 1):
        for sy in (-1, 1):
            there = exists(sx, sy)
            diagonal = diagonal + jnp.where(there, 1, 0)

            @pl.when(there)
            def _(sx=sx, sy=sy):
                pl.semaphore_signal(barrier, inc=1, device_id=(ix + sx, iy + sy), device_id_type=MESH)

    def turn_in(x, _):
        for y in range(size_y):
            xs[x + 1, y + 1] = x_in[pl.ds(x * size_y + y, vectors, stride=cells), :]
        return 0

    lax.fori_loop(0, size_x, turn_in, 0)
    k_stage[0] = cond_in[:, size_y - 1, :]
    k_stage[1] = cond_in[:, 0, :]

    pl.semaphore_wait(barrier, nx - 1 + ny - 1 + diagonal)

    inner_x, inner_y = pl.ds(1, size_x), pl.ds(1, size_y)
    first = [
        (k_stage.at[0], k_side.at[2], 0, 1, 0),
        (k_stage.at[1], k_side.at[3], 0, -1, 1),
        (cond_in.at[size_x - 1], k_side.at[0], 1, 0, 2),
        (cond_in.at[0], k_side.at[1], -1, 0, 3),
        (xs.at[inner_x, size_y], xs.at[inner_x, 0], 0, 1, 4),
        (xs.at[inner_x, 1], xs.at[inner_x, size_y + 1], 0, -1, 5),
        (xs.at[size_x, inner_y], xs.at[0, inner_y], 1, 0, 6),
        (xs.at[1, inner_y], xs.at[size_x + 1, inner_y], -1, 0, 7),
        (xs.at[size_x, size_y], xs.at[0, 0], 1, 1, 8),
        (xs.at[size_x, 1], xs.at[0, size_y + 1], 1, -1, 9),
    ]
    start(first)

    lane = lax.broadcasted_iota(jnp.int32, (size_y, depth), 1)
    piece = lane // (depth // blocks)
    for o in range(DIAG):
        dz = lower_offsets[o][2]
        keep = jnp.zeros((size_y, depth), F32)
        for b in range(blocks):
            keep = jnp.where(piece == b, pattern_in[b, o].astype(F32), keep)
        if dz:
            keep = jnp.where(lane == (0 if dz < 0 else depth - 1), 0.0, keep)

        def fill(x, _, o=o, dz=dz, keep=keep):
            term = lower_in[o, x] * keep
            lm[o, x + 1, pl.ds(2, size_y), :] = term
            lp[o, x] = pltpu.roll(term, dz % depth, 1) if dz else term
            return 0

        lax.fori_loop(0, size_x, fill, 0)

    def fill_diag(x, _):
        lm[DIAG, x + 1, pl.ds(2, size_y), :] = diag_in[x]
        return 0

    lax.fori_loop(0, size_x, fill_diag, 0)

    def rims(o, _):
        for x in range(size_x + 2):
            if x in (0, size_x + 1):
                lm[o, x] = jnp.zeros((lm.shape[2], depth), F32)
            else:
                lm[o, x, pl.ds(0, 2), :] = jnp.zeros((2, depth), F32)
                lm[o, x, pl.ds(size_y + 2, 2), :] = jnp.zeros((2, depth), F32)
        return 0

    lax.fori_loop(0, DIAG + 1, rims, 0)
    for y in range(size_y + 4):
        pr[0, y] = zero_col
        pr[size_x + 1, y] = zero_col
    for x in range(1, size_x + 1):
        for y in (0, 1, size_y + 2, size_y + 3):
            pr[x, y] = zero_col
    for y in range(size_y + 2):
        adv[0, y] = zero_col
        adv[size_x + 1, y] = zero_col
    for x in range(1, size_x + 1):
        adv[x, 0] = zero_col
        adv[x, size_y + 1] = zero_col

    row = lax.broadcasted_iota(jnp.int32, (vectors, depth), 0)
    step_col, mom_col = zero_col, zero_col
    for k in range(vectors):
        step_col = jnp.where(row == k, step_in[k], step_col)
        mom_col = jnp.where(row == k, mom_in[k], mom_col)

    wait_recv(first[:4])
    row8 = lax.broadcasted_iota(jnp.int32, (size_y, depth), 0)

    def faces(x, _):
        here = cond_in[x]
        below = jnp.where(x == 0, k_side[0], cond_in[jnp.maximum(x - 1, 0)])
        above = jnp.where(x == size_x - 1, k_side[1], cond_in[jnp.minimum(x + 1, size_x - 1)])
        left = jnp.where(row8 == 0, k_side[2, pl.ds(x, 1), :], pltpu.roll(here, 1, 0))
        right = jnp.where(row8 == size_y - 1, k_side[3, pl.ds(x, 1), :], pltpu.roll(here, size_y - 1, 0))
        back = jnp.where(lane == 0, 0.0, pltpu.roll(here, 1, 1))
        front = jnp.where(lane == depth - 1, 0.0, pltpu.roll(here, depth - 1, 1))
        total = None
        for i, near in enumerate((below, above, left, right, back, front)):
            face = 0.5 * (here + near)
            total = face if total is None else total + face
            if i == 4:
                face = jnp.where(lane == 0, 0.0, face)
            if i == 5:
                face = jnp.where(lane == depth - 1, 0.0, face)
            coef[i + 1, x] = face
        coef[0, x] = total
        return 0

    lax.fori_loop(0, size_x, faces, 0)

    def stiffness(buf, x, y):
        centre = buf[x + 1, y + 1]

        def c(i):
            return coef[i, x, pl.ds(y, 1), :]

        return (
            c(0) * centre
            - c(1) * buf[x, y + 1] - c(2) * buf[x + 2, y + 1]
            - c(3) * buf[x + 1, y] - c(4) * buf[x + 1, y + 2]
            - c(5) * pltpu.roll(centre, 1, 1) - c(6) * pltpu.roll(centre, depth - 1, 1)
        )

    wait_recv(first[4:])

    def images(x, sums):
        sum_xx, sum_xa = sums
        for y in range(size_y):
            centre = xs[x + 1, y + 1]
            image = stiffness(xs, x, y)
            im[x + 1, y + 1] = image
            sum_xx = sum_xx + centre * centre
            sum_xa = sum_xa + centre * image
        return sum_xx, sum_xa

    sum_xx, sum_xa = lax.fori_loop(0, size_x, images, (zero_col, zero_col))
    lane16 = lax.broadcasted_iota(jnp.int32, (vectors, depth), 1)
    both = jnp.where(
        lane16 < depth // 2,
        jnp.sum(sum_xx, axis=1, keepdims=True), jnp.sum(sum_xa, axis=1, keepdims=True),
    )
    reduce_start(q_x, 0, both)
    second = [
        (im.at[inner_x, size_y], im.at[inner_x, 0], 0, 1, 10),
        (im.at[inner_x, 1], im.at[inner_x, size_y + 1], 0, -1, 11),
        (im.at[size_x, inner_y], im.at[0, inner_y], 1, 0, 12),
        (im.at[size_x, size_y], im.at[0, 0], 1, 1, 13),
        (im.at[size_x, 1], im.at[0, size_y + 1], 1, -1, 14),
    ]
    start(second)
    both = reduce_finish(q_x, q_y, 0)
    quotient = both[:, depth // 2 : depth // 2 + 1] * scale / (both[:, 0:1] * scale + 1e-06)
    quotient = jnp.broadcast_to(quotient, (vectors, depth))
    wait_recv(second)

    def gradients(x, _):
        for y in range(size_y + 2):
            gr[x, y] = im[x, y] - quotient * xs[x, y]
        return 0

    lax.fori_loop(0, size_x + 1, gradients, 0)

    def products(x, _):
        for y in range(size_y):
            parts = {0: diag_in[x, pl.ds(y, 1), :] * gr[x + 1, y + 1], -1: zero_col, 1: zero_col}
            for o, (dx, dy, dz) in enumerate(lower_offsets):
                parts[dz] = parts[dz] + lp[o, x, pl.ds(y, 1), :] * gr[x + 1 + dx, y + 1 + dy]
            pr[x + 1, y + 2] = (
                parts[0] + pltpu.roll(parts[-1], 1, 1) + pltpu.roll(parts[1], depth - 1, 1)
            )
        return 0

    lax.fori_loop(0, size_x, products, 0)

    def target(x, y):
        parts = {0: lm[DIAG, x, pl.ds(y + 1, 1), :] * pr[x, y + 1], -1: zero_col, 1: zero_col}
        for o, (dx, dy, dz) in enumerate(lower_offsets):
            parts[dz] = parts[dz] + lm[o, x - dx, pl.ds(y + 1 - dy, 1), :] * pr[x - dx, y + 1 - dy]
        pt[x, y] = parts[0] + pltpu.roll(parts[-1], depth - 1, 1) + pltpu.roll(parts[1], 1, 1)

    for y in range(size_y + 2):
        target(0, y)

    def rim_targets(x, _):
        target(x, 0)
        target(x, size_y + 1)
        return 0

    lax.fori_loop(1, size_x + 1, rim_targets, 0)
    third = [
        (pt.at[inner_x, 0], recv_y0, 0, -1, 15),
        (pt.at[inner_x, size_y + 1], recv_y1, 0, 1, 16),
        (pt.at[0, inner_y], recv_x, -1, 0, 17),
        (pt.at[0, 0], recv_c.at[0], -1, -1, 18),
        (pt.at[0, size_y + 1], recv_c.at[1], -1, 1, 19),
    ]
    start(third)

    def own_targets(x, _):
        for y in range(1, size_y + 1):
            target(x, y)
        return 0

    lax.fori_loop(1, size_x + 1, own_targets, 0)
    wait_recv(third)
    for y in range(size_y):
        pt[size_x, y + 1] = pt[size_x, y + 1] + recv_x[y]
    for x in range(size_x):
        pt[x + 1, size_y] = pt[x + 1, size_y] + recv_y0[x]
        pt[x + 1, 1] = pt[x + 1, 1] + recv_y1[x]
    pt[size_x, size_y] = pt[size_x, size_y] + recv_c[0]
    pt[size_x, 1] = pt[size_x, 1] + recv_c[1]

    def at_column(index):
        return pl.ds(pl.multiple_of(index * depth, depth), depth)

    def put(buf, base, index, value):
        for i, part in enumerate(split3(value)):
            buf[base + i * vectors : base + (i + 1) * vectors, at_column(index)] = part

    def advance(x, _):
        for y in range(size_y):
            spot = pl.ds(x * size_y + y, vectors, stride=cells)
            direction = pt[x + 1, y + 1] + mom_col * old_in[spot, :]
            dir_out[spot, :] = direction
            advanced = xs[x + 1, y + 1] + step_col * direction
            adv[x + 1, y + 1] = advanced
            put(ab, 0, x * size_y + y, advanced)
        return 0

    lax.fori_loop(0, size_x, advance, 0)
    fourth = [
        (adv.at[inner_x, 1], halo_y, 0, -1, 20),
        (adv.at[1, inner_y], halo_x, -1, 0, 21),
    ]
    start(fourth)

    def advanced_images(x, _):
        for y in range(size_y):
            put(ab, 3 * vectors, x * size_y + y, stiffness(adv, x, y))
        return 0

    lax.fori_loop(0, size_x, advanced_images, 0)
    nt = (((1,), (1,)), ((), ()))
    grams = lax.dot_general(ab[0 : 3 * vectors, :], ab[...], nt, preferred_element_type=F32)
    wait_recv(fourth)
    for y in range(size_y):
        put(abh, 0, y, adv[size_x, y + 1])
        put(abh, 3 * vectors, y, -coef[2, size_x - 1, pl.ds(y, 1), :] * halo_x[y])
    for x in range(size_x):
        put(abh, 0, size_y + x, adv[x + 1, size_y])
        put(abh, 3 * vectors, size_y + x, -coef[4, x, pl.ds(size_y - 1, 1), :] * halo_y[x])
    crossed = lax.dot_general(abh[...], abh[...], nt, preferred_element_type=F32)

    def rows(array, base):
        return (
            array[base : base + vectors]
            + array[base + vectors : base + 2 * vectors]
            + array[base + 2 * vectors : base + 3 * vectors]
        )

    def wide(array):
        return jnp.concatenate([array, jnp.zeros((vectors, depth - 6 * vectors), F32)], axis=1)

    def lanes(array):
        return (
            array + pltpu.roll(array, depth - vectors, 1) + pltpu.roll(array, depth - 2 * vectors, 1)
        )

    main = lanes(wide(rows(grams, 0)))
    upper = lanes(wide(rows(crossed, 0)))
    lower = lanes(wide(rows(crossed, 3 * vectors)))
    stiff = pltpu.roll(main + upper, depth - 2 * vectors, 1) + pltpu.roll(lower, vectors, 1)
    packed = jnp.where(lane16 < vectors, main, jnp.where(lane16 < 2 * vectors, stiff, 0.0))
    reduce_start(g_x, 1, packed)
    packed = reduce_finish(g_x, g_y, 1) * scale

    aug = packed + jnp.where(row == lane16, 1e-05, 0.0)
    aug = aug + jnp.where(row + 2 * vectors == lane16, 1.0, 0.0)
    for j in range(vectors - 1):
        ratio = aug[:, j : j + 1] / aug[j : j + 1, j : j + 1]
        aug = aug - jnp.where(row > j, ratio * aug[j : j + 1, :], 0.0)
    pivots = jnp.sum(jnp.where(row == lane16, aug, 0.0), axis=1, keepdims=True)
    aug = aug / jnp.sqrt(pivots)
    inverse = aug[:, 2 * vectors : 3 * vectors]
    ray_out[...] = lax.dot_general(
        aug[:, vectors : 2 * vectors], inverse, nt,
        preferred_element_type=F32, precision=lax.Precision.HIGHEST,
    )
    weights = jnp.concatenate(
        [jnp.concatenate([part.astype(F32)] * 3, axis=1) for part in split3(inverse)], axis=0
    ).astype(BF16)

    def rotate(x, _):
        wide_part = pl.ds(pl.multiple_of(x * size_y * depth, depth), size_y * depth)
        mixed = rows(
            jnp.dot(weights, ab[0 : 3 * vectors, wide_part], preferred_element_type=F32), 0
        )
        for y in range(size_y):
            next_out[pl.ds(x * size_y + y, vectors, stride=cells), :] = mixed[
                :, y * depth : (y + 1) * depth
            ]
        return 0

    lax.fori_loop(0, size_x, rotate, 0)
    for items in (first, second, third, fourth):
        wait_send(items)


def per_device(
    x_block, old_direction, conductivity, fsai_diagonal, fsai_lower, pattern, step_size, momentum
):
    vectors, size_x, size_y, size_z = x_block.shape
    nx, ny = lax.axis_size("gx"), lax.axis_size("gy")
    cells = size_x * size_y
    scale = 1.0 / (cells * size_z * nx * ny)
    flat = (vectors * cells, size_z)
    column = (vectors, size_z)
    vmem = pl.BlockSpec(memory_space=pltpu.VMEM)
    smem = pl.BlockSpec(memory_space=pltpu.SMEM)

    def padded(rx, ry):
        return pltpu.VMEM((size_x + 2 * rx, size_y + 2 * ry) + column, F32)

    terms = fsai_lower.shape[0] + 1
    x_next, direction, rayleigh = pl.pallas_call(
        functools.partial(kernel, nx, ny, scale),
        out_shape=[
            jax.ShapeDtypeStruct(flat, F32),
            jax.ShapeDtypeStruct(flat, F32),
            jax.ShapeDtypeStruct((vectors, vectors), F32),
        ],
        in_specs=[vmem] * 5 + [smem] * 3,
        out_specs=[vmem] * 3,
        scratch_shapes=[
            padded(1, 1), padded(1, 1), padded(1, 1), padded(1, 2), padded(1, 1), padded(1, 1),
            pltpu.VMEM((size_y,) + column, F32),
            pltpu.VMEM((size_x,) + column, F32),
            pltpu.VMEM((size_x,) + column, F32),
            pltpu.VMEM((2,) + column, F32),
            pltpu.VMEM((size_y,) + column, F32),
            pltpu.VMEM((size_x,) + column, F32),
            pltpu.VMEM((4, size_y, size_z), F32),
            pltpu.VMEM((2, size_x, size_z), F32),
            pltpu.VMEM((7, size_x, size_y, size_z), F32),
            pltpu.VMEM((terms, size_x + 2, size_y + 8, size_z), F32),
            pltpu.VMEM((terms - 1, size_x, size_y, size_z), F32),
            pltpu.VMEM((6 * vectors, cells * size_z), BF16),
            pltpu.VMEM((6 * vectors, (size_x + size_y) * size_z), BF16),
            pltpu.VMEM((nx,) + column, F32),
            pltpu.VMEM((ny,) + column, F32),
            pltpu.VMEM((nx,) + column, F32),
            pltpu.VMEM((ny,) + column, F32),
            pltpu.SemaphoreType.DMA((22,)),
            pltpu.SemaphoreType.DMA((22,)),
            pltpu.SemaphoreType.DMA((2, nx)),
            pltpu.SemaphoreType.DMA((2, nx)),
            pltpu.SemaphoreType.DMA((2, ny)),
            pltpu.SemaphoreType.DMA((2, ny)),
        ],
        compiler_params=pltpu.CompilerParams(
            collective_id=0, has_side_effects=True, vmem_limit_bytes=48 * 1024 * 1024
        ),
    )(
        x_block.reshape(flat), old_direction.reshape(flat), conductivity, fsai_diagonal,
        fsai_lower, pattern, step_size, momentum,
    )
    return x_next.reshape(x_block.shape), direction.reshape(x_block.shape), rayleigh


def solution(mesh):
    placed = (
        P(None, "gx", "gy", None),
        P(None, "gx", "gy", None),
        P("gx", "gy", None),
        P("gx", "gy", None),
        P(None, "gx", "gy", None),
        P(),
        P(),
        P(),
    )
    return jax.shard_map(
        per_device,
        mesh=mesh,
        in_specs=placed,
        out_specs=(P(None, "gx", "gy", None), P(None, "gx", "gy", None), P()),
        check_vma=False,
    )
```

```python
import functools

import jax
import jax.numpy as jnp
from jax import lax
from jax.experimental import pallas as pl
from jax.experimental.pallas import tpu as pltpu
from jax.sharding import PartitionSpec as P

MESH = pl.DeviceIdType.MESH
F32 = jnp.float32
BF16 = jnp.bfloat16

lower_offsets = [
    (a, b, c) for a in (-1, 0, 1) for b in (-1, 0, 1) for c in (-1, 0, 1) if (a, b, c) < (0, 0, 0)
]
DIAG = len(lower_offsets)
SIDES = [(1, 0), (-1, 0), (0, 1), (0, -1)]


def split3(value):
    high = value.astype(BF16)
    rest = value - high.astype(F32)
    middle = rest.astype(BF16)
    low = (rest - middle.astype(F32)).astype(BF16)
    return high, middle, low


def kernel(
    nx, ny, scale,
    x_hbm, old_hbm, cond_hbm, diag_hbm, lower_hbm, pattern_hbm, step_hbm, mom_hbm,
    next_out, dir_out, ray_out,
    x_in, old_in, cond_in, diag_in, lower_in, pattern_in, step_in, mom_in,
    xs, im, pr, ptx, pt, adv,
    rx_x, rx_y0, rx_y1, rx_c, recv_x, recv_y0, recv_y1, recv_c, halo_x, halo_y,
    k_side, k_stage, coef, lm, lp,
    ab, abh, q_x, q_y, g_x, g_y, s_x, s_y,
    load_sem, send_sem, recv_sem, send_x, recv_gx, send_y, recv_gy,
):
    loads = [
        pltpu.make_async_copy(src, dst, load_sem.at[i])
        for i, (src, dst) in enumerate((
            (x_hbm, x_in), (cond_hbm, cond_in), (pattern_hbm, pattern_in), (lower_hbm, lower_in),
            (diag_hbm, diag_in), (step_hbm, step_in), (mom_hbm, mom_in), (old_hbm, old_in),
        ))
    ]
    for load in loads:
        load.start()
    ix, iy = lax.axis_index("gx"), lax.axis_index("gy")
    size_x, size_y = cond_in.shape[0], cond_in.shape[1]
    depth = cond_in.shape[2]
    vectors = xs.shape[2]
    cells = size_x * size_y
    blocks = pattern_in.shape[0]
    zero_col = jnp.zeros((vectors, depth), F32)
    zero_tile = jnp.zeros((size_y, depth), F32)

    def exists(sx, sy):
        found = None
        for ok, step in (
            (ix + 1 < nx, sx > 0), (ix > 0, sx < 0), (iy + 1 < ny, sy > 0), (iy > 0, sy < 0)
        ):
            if step:
                found = ok if found is None else jnp.logical_and(found, ok)
        return found

    def copy_of(item):
        src, dst, sx, sy, slot = item
        return pltpu.make_async_remote_copy(
            src_ref=src, dst_ref=dst, send_sem=send_sem.at[slot], recv_sem=recv_sem.at[slot],
            device_id=(ix + sx, iy + sy), device_id_type=MESH,
        )

    def start(items):
        for item in items:
            @pl.when(exists(item[2], item[3]))
            def _(item=item):
                copy_of(item).start()

    def wait_recv(items):
        for item in items:
            @pl.when(exists(-item[2], -item[3]))
            def _(item=item):
                copy_of(item).wait_recv()

    def wait_send(items):
        for item in items:
            @pl.when(exists(item[2], item[3]))
            def _(item=item):
                copy_of(item).wait_send()

    def group_start(buf, turn, n, me, place, sends, recvs):
        for s in range(1, n):
            peer = lax.rem(me + s, n)
            pltpu.make_async_remote_copy(
                src_ref=buf.at[me], dst_ref=buf.at[me], send_sem=sends.at[turn, s],
                recv_sem=recvs.at[turn, s], device_id=place(peer), device_id_type=MESH,
            ).start()

    def group_wait(buf, turn, n, me, place, sends, recvs):
        for s in range(1, n):
            peer = lax.rem(me + n - s, n)
            pltpu.make_async_remote_copy(
                src_ref=buf.at[peer], dst_ref=buf.at[peer], send_sem=sends.at[turn, s],
                recv_sem=recvs.at[turn, s], device_id=place(peer), device_id_type=MESH,
            ).wait()

    def along_x(peer):
        return (peer, iy)

    def along_y(peer):
        return (ix, peer)

    def reduce_start(buf_x, turn, tile):
        buf_x[ix] = tile
        group_start(buf_x, turn, nx, ix, along_x, send_x, recv_gx)

    def reduce_middle(buf_x, buf_y, turn):
        group_wait(buf_x, turn, nx, ix, along_x, send_x, recv_gx)
        total = buf_x[0]
        for i in range(1, nx):
            total = total + buf_x[i]
        buf_y[iy] = total
        group_start(buf_y, turn, ny, iy, along_y, send_y, recv_gy)

    def reduce_finish(buf_y, turn):
        group_wait(buf_y, turn, ny, iy, along_y, send_y, recv_gy)
        total = buf_y[0]
        for i in range(1, ny):
            total = total + buf_y[i]
        return total

    for buf in (xs, im):
        for y in range(size_y + 2):
            buf[0, y] = zero_col
            buf[size_x + 1, y] = zero_col
        for x in range(1, size_x + 1):
            buf[x, 0] = zero_col
            buf[x, size_y + 1] = zero_col
    for i in range(4):
        k_side[i] = zero_tile
    for buf in (rx_x, rx_y0, rx_y1, rx_c, recv_x, recv_y0, recv_y1, recv_c, halo_x, halo_y):
        for i in range(buf.shape[0]):
            buf[i] = zero_col

    barrier = pltpu.get_barrier_semaphore()
    for s in range(1, nx):
        pl.semaphore_signal(barrier, inc=1, device_id=along_x(lax.rem(ix + s, nx)), device_id_type=MESH)
    for s in range(1, ny):
        pl.semaphore_signal(barrier, inc=1, device_id=along_y(lax.rem(iy + s, ny)), device_id_type=MESH)
    diagonal = 0
    for sx in (-1, 1):
        for sy in (-1, 1):
            there = exists(sx, sy)
            diagonal = diagonal + jnp.where(there, 1, 0)

            @pl.when(there)
            def _(sx=sx, sy=sy):
                pl.semaphore_signal(barrier, inc=1, device_id=(ix + sx, iy + sy), device_id_type=MESH)

    loads[0].wait()
    loads[1].wait()

    def turn_in(x, _):
        for y in range(size_y):
            xs[x + 1, y + 1] = x_in[pl.ds(x * size_y + y, vectors, stride=cells), :]
        return 0

    lax.fori_loop(0, size_x, turn_in, 0)
    k_stage[0] = cond_in[:, size_y - 1, :]
    k_stage[1] = cond_in[:, 0, :]

    pl.semaphore_wait(barrier, nx - 1 + ny - 1 + diagonal)

    inner_x, inner_y = pl.ds(1, size_x), pl.ds(1, size_y)
    first = [
        (k_stage.at[0], k_side.at[2], 0, 1, 0),
        (k_stage.at[1], k_side.at[3], 0, -1, 1),
        (cond_in.at[size_x - 1], k_side.at[0], 1, 0, 2),
        (cond_in.at[0], k_side.at[1], -1, 0, 3),
        (xs.at[inner_x, size_y], xs.at[inner_x, 0], 0, 1, 4),
        (xs.at[inner_x, 1], xs.at[inner_x, size_y + 1], 0, -1, 5),
        (xs.at[size_x, inner_y], xs.at[0, inner_y], 1, 0, 6),
        (xs.at[1, inner_y], xs.at[size_x + 1, inner_y], -1, 0, 7),
        (xs.at[size_x, size_y], xs.at[0, 0], 1, 1, 8),
        (xs.at[size_x, 1], xs.at[0, size_y + 1], 1, -1, 9),
    ]
    start(first)

    for load in loads[2:]:
        load.wait()
    lane = lax.broadcasted_iota(jnp.int32, (size_y, depth), 1)
    piece = lane // (depth // blocks)
    for o in range(DIAG):
        dz = lower_offsets[o][2]
        keep = jnp.zeros((size_y, depth), F32)
        for b in range(blocks):
            keep = jnp.where(piece == b, pattern_in[b, o].astype(F32), keep)
        if dz:
            keep = jnp.where(lane == (0 if dz < 0 else depth - 1), 0.0, keep)

        for x in range(size_x):
            term = lower_in[o, x] * keep
            lm[o, x + 1, pl.ds(2, size_y), :] = term
            lp[o, x] = pltpu.roll(term, dz % depth, 1) if dz else term

    for x in range(size_x):
        lm[DIAG, x + 1, pl.ds(2, size_y), :] = diag_in[x]

    def rims(o, _):
        for x in range(size_x + 2):
            if x in (0, size_x + 1):
                lm[o, x] = jnp.zeros((lm.shape[2], depth), F32)
            else:
                lm[o, x, pl.ds(0, 2), :] = jnp.zeros((2, depth), F32)
                lm[o, x, pl.ds(size_y + 2, 2), :] = jnp.zeros((2, depth), F32)
        return 0

    lax.fori_loop(0, DIAG + 1, rims, 0)
    for y in range(size_y + 4):
        pr[0, y] = zero_col
        pr[size_x + 1, y] = zero_col
    for x in range(1, size_x + 1):
        for y in (0, 1, size_y + 2, size_y + 3):
            pr[x, y] = zero_col
    for y in range(size_y + 2):
        adv[0, y] = zero_col
        adv[size_x + 1, y] = zero_col
    for x in range(1, size_x + 1):
        adv[x, 0] = zero_col
        adv[x, size_y + 1] = zero_col

    row = lax.broadcasted_iota(jnp.int32, (vectors, depth), 0)
    step_col, mom_col = zero_col, zero_col
    for k in range(vectors):
        step_col = jnp.where(row == k, step_in[k], step_col)
        mom_col = jnp.where(row == k, mom_in[k], mom_col)

    wait_recv(first[:4])
    row8 = lax.broadcasted_iota(jnp.int32, (size_y, depth), 0)

    for x in range(size_x):
        here = cond_in[x]
        below = k_side[0] if x == 0 else cond_in[x - 1]
        above = k_side[1] if x == size_x - 1 else cond_in[x + 1]
        left = jnp.where(row8 == 0, k_side[2, pl.ds(x, 1), :], pltpu.roll(here, 1, 0))
        right = jnp.where(row8 == size_y - 1, k_side[3, pl.ds(x, 1), :], pltpu.roll(here, size_y - 1, 0))
        back = jnp.where(lane == 0, 0.0, pltpu.roll(here, 1, 1))
        front = jnp.where(lane == depth - 1, 0.0, pltpu.roll(here, depth - 1, 1))
        total = None
        for i, near in enumerate((below, above, left, right, back, front)):
            face = 0.5 * (here + near)
            total = face if total is None else total + face
            if i == 4:
                face = jnp.where(lane == 0, 0.0, face)
            if i == 5:
                face = jnp.where(lane == depth - 1, 0.0, face)
            coef[i + 1, x] = face
        coef[0, x] = total

    def stiffness(buf, x, y):
        centre = buf[x + 1, y + 1]

        def c(i):
            return coef[i, x, pl.ds(y, 1), :]

        return (
            c(0) * centre
            - c(1) * buf[x, y + 1] - c(2) * buf[x + 2, y + 1]
            - c(3) * buf[x + 1, y] - c(4) * buf[x + 1, y + 2]
            - c(5) * pltpu.roll(centre, 1, 1) - c(6) * pltpu.roll(centre, depth - 1, 1)
        )

    wait_recv(first[4:])

    def images(x, sums):
        sum_xx, sum_xa = sums
        for y in range(size_y):
            centre = xs[x + 1, y + 1]
            image = stiffness(xs, x, y)
            im[x + 1, y + 1] = image
            sum_xx = sum_xx + centre * centre
            sum_xa = sum_xa + centre * image
        return sum_xx, sum_xa

    sum_xx, sum_xa = lax.fori_loop(0, size_x, images, (zero_col, zero_col))
    lane16 = lax.broadcasted_iota(jnp.int32, (vectors, depth), 1)
    both = jnp.where(
        lane16 < depth // 2,
        jnp.sum(sum_xx, axis=1, keepdims=True), jnp.sum(sum_xa, axis=1, keepdims=True),
    )
    second = [
        (im.at[inner_x, size_y], im.at[inner_x, 0], 0, 1, 10),
        (im.at[inner_x, 1], im.at[inner_x, size_y + 1], 0, -1, 11),
        (im.at[size_x, inner_y], im.at[0, inner_y], 1, 0, 12),
        (im.at[size_x, size_y], im.at[0, 0], 1, 1, 13),
        (im.at[size_x, 1], im.at[0, size_y + 1], 1, -1, 14),
    ]
    start(second)
    reduce_start(q_x, 0, both)

    def factor(buf):
        def products(x, _):
            for y in range(size_y):
                parts = {0: diag_in[x, pl.ds(y, 1), :] * buf[x + 1, y + 1], -1: zero_col, 1: zero_col}
                for o, (dx, dy, dz) in enumerate(lower_offsets):
                    parts[dz] = parts[dz] + lp[o, x, pl.ds(y, 1), :] * buf[x + 1 + dx, y + 1 + dy]
                pr[x + 1, y + 2] = (
                    parts[0] + pltpu.roll(parts[-1], 1, 1) + pltpu.roll(parts[1], depth - 1, 1)
                )
            return 0

        lax.fori_loop(0, size_x, products, 0)

    def transposed(out, arrivals, slot):
        def target(x, y):
            parts = {0: lm[DIAG, x, pl.ds(y + 1, 1), :] * pr[x, y + 1], -1: zero_col, 1: zero_col}
            for o, (dx, dy, dz) in enumerate(lower_offsets):
                parts[dz] = parts[dz] + lm[o, x - dx, pl.ds(y + 1 - dy, 1), :] * pr[x - dx, y + 1 - dy]
            out[x, y] = parts[0] + pltpu.roll(parts[-1], depth - 1, 1) + pltpu.roll(parts[1], 1, 1)

        for y in range(size_y + 2):
            target(0, y)

        def rim_targets(x, _):
            target(x, 0)
            target(x, size_y + 1)
            return 0

        lax.fori_loop(1, size_x + 1, rim_targets, 0)
        to_x, to_y0, to_y1, to_c = arrivals
        items = [
            (out.at[inner_x, 0], to_y0, 0, -1, slot),
            (out.at[inner_x, size_y + 1], to_y1, 0, 1, slot + 1),
            (out.at[0, inner_y], to_x, -1, 0, slot + 2),
            (out.at[0, 0], to_c.at[0], -1, -1, slot + 3),
            (out.at[0, size_y + 1], to_c.at[1], -1, 1, slot + 4),
        ]
        start(items)

        def own_targets(x, _):
            for y in range(1, size_y + 1):
                target(x, y)
            return 0

        lax.fori_loop(1, size_x + 1, own_targets, 0)
        return items

    def gather(out, arrivals, items):
        wait_recv(items)
        to_x, to_y0, to_y1, to_c = arrivals
        for y in range(size_y):
            out[size_x, y + 1] = out[size_x, y + 1] + to_x[y]
        for x in range(size_x):
            out[x + 1, size_y] = out[x + 1, size_y] + to_y0[x]
            out[x + 1, 1] = out[x + 1, 1] + to_y1[x]
        out[size_x, size_y] = out[size_x, size_y] + to_c[0]
        out[size_x, 1] = out[size_x, 1] + to_c[1]

    arrivals_x = (rx_x, rx_y0, rx_y1, rx_c)
    arrivals = (recv_x, recv_y0, recv_y1, recv_c)
    factor(xs)
    third_x = transposed(ptx, arrivals_x, 22)
    reduce_middle(q_x, q_y, 0)
    wait_recv(second)
    factor(im)
    third = transposed(pt, arrivals, 15)
    gather(ptx, arrivals_x, third_x)
    both = reduce_finish(q_y, 0)
    quotient = both[:, depth // 2 : depth // 2 + 1] * scale / (both[:, 0:1] * scale + 1e-06)
    quotient = jnp.broadcast_to(quotient, (vectors, depth))
    gather(pt, arrivals, third)

    def at_column(index):
        return pl.ds(pl.multiple_of(index * depth, depth), depth)

    def put(buf, base, index, value):
        for i, part in enumerate(split3(value)):
            buf[base + i * vectors : base + (i + 1) * vectors, at_column(index)] = part

    def advance(x, _):
        for y in range(size_y):
            spot = pl.ds(x * size_y + y, vectors, stride=cells)
            direction = (pt[x + 1, y + 1] - quotient * ptx[x + 1, y + 1]) + mom_col * old_in[spot, :]
            dir_out[spot, :] = direction
            advanced = xs[x + 1, y + 1] + step_col * direction
            adv[x + 1, y + 1] = advanced
            put(ab, 0, x * size_y + y, advanced)
        return 0

    lax.fori_loop(0, size_x, advance, 0)
    fourth = [
        (adv.at[inner_x, 1], halo_y, 0, -1, 20),
        (adv.at[1, inner_y], halo_x, -1, 0, 21),
    ]
    start(fourth)
    nt = (((1,), (1,)), ((), ()))
    third_rows = 3 * vectors

    def collect(array):
        return sum(
            array[i * vectors : (i + 1) * vectors, j * vectors : (j + 1) * vectors]
            for i in range(3) for j in range(3)
        )

    def as_tile(array):
        return jnp.concatenate([array, jnp.zeros((vectors, depth - vectors), F32)], axis=1)

    gram = collect(lax.dot_general(
        ab[0:third_rows, :], ab[0:third_rows, :], nt, preferred_element_type=F32
    ))
    reduce_start(g_x, 1, as_tile(gram))

    def advanced_images(x, _):
        for y in range(size_y):
            put(ab, third_rows, x * size_y + y, stiffness(adv, x, y))
        return 0

    lax.fori_loop(0, size_x, advanced_images, 0)
    reduce_middle(g_x, g_y, 1)
    stiff = collect(lax.dot_general(
        ab[0:third_rows, :], ab[third_rows:, :], nt, preferred_element_type=F32
    ))
    wait_recv(fourth)
    for y in range(size_y):
        put(abh, 0, y, adv[size_x, y + 1])
        put(abh, third_rows, y, -coef[2, size_x - 1, pl.ds(y, 1), :] * halo_x[y])
    for x in range(size_x):
        put(abh, 0, size_y + x, adv[x + 1, size_y])
        put(abh, third_rows, size_y + x, -coef[4, x, pl.ds(size_y - 1, 1), :] * halo_y[x])
    crossed = lax.dot_general(abh[...], abh[...], nt, preferred_element_type=F32)
    stiff = stiff + collect(crossed[0:third_rows, third_rows:]) + collect(crossed[third_rows:, 0:third_rows])
    reduce_start(s_x, 2, as_tile(stiff))

    aug = reduce_finish(g_y, 1) * scale + jnp.where(row == lane16, 1e-05, 0.0)
    aug = aug + jnp.where(row + vectors == lane16, 1.0, 0.0)
    for j in range(vectors - 1):
        ratio = aug[:, j : j + 1] / aug[j : j + 1, j : j + 1]
        aug = aug - jnp.where(row > j, ratio * aug[j : j + 1, :], 0.0)
    pivots = jnp.sum(jnp.where(row == lane16, aug, 0.0), axis=1, keepdims=True)
    aug = aug / jnp.sqrt(pivots)
    inverse = aug[:, vectors : 2 * vectors]
    reduce_middle(s_x, s_y, 2)
    weights = jnp.concatenate(
        [jnp.concatenate([part.astype(F32)] * 3, axis=1) for part in split3(inverse)], axis=0
    ).astype(BF16)

    def rows(array):
        return array[:vectors] + array[vectors : 2 * vectors] + array[2 * vectors :]

    def rotate(x, _):
        wide_part = pl.ds(pl.multiple_of(x * size_y * depth, depth), size_y * depth)
        mixed = rows(
            jnp.dot(weights, ab[0 : 3 * vectors, wide_part], preferred_element_type=F32)
        )
        for y in range(size_y):
            next_out[pl.ds(x * size_y + y, vectors, stride=cells), :] = mixed[
                :, y * depth : (y + 1) * depth
            ]
        return 0

    lax.fori_loop(0, size_x, rotate, 0)
    stiff = (reduce_finish(s_y, 2) * scale)[:, 0:vectors]
    highest = lax.Precision.HIGHEST
    half = jnp.dot(inverse, stiff, preferred_element_type=F32, precision=highest)
    ray_out[...] = lax.dot_general(half, inverse, nt, preferred_element_type=F32, precision=highest)
    for items in (first, second, third_x, third, fourth):
        wait_send(items)


def per_device(
    x_block, old_direction, conductivity, fsai_diagonal, fsai_lower, pattern, step_size, momentum
):
    vectors, size_x, size_y, size_z = x_block.shape
    nx, ny = lax.axis_size("gx"), lax.axis_size("gy")
    cells = size_x * size_y
    scale = 1.0 / (cells * size_z * nx * ny)
    flat = (vectors * cells, size_z)
    column = (vectors, size_z)
    vmem = pl.BlockSpec(memory_space=pltpu.VMEM)
    hbm = pl.BlockSpec(memory_space=pltpu.HBM)

    def padded(rx, ry):
        return pltpu.VMEM((size_x + 2 * rx, size_y + 2 * ry) + column, F32)

    terms = fsai_lower.shape[0] + 1
    x_next, direction, rayleigh = pl.pallas_call(
        functools.partial(kernel, nx, ny, scale),
        out_shape=[
            jax.ShapeDtypeStruct(flat, F32),
            jax.ShapeDtypeStruct(flat, F32),
            jax.ShapeDtypeStruct((vectors, vectors), F32),
        ],
        in_specs=[hbm] * 8,
        out_specs=[vmem] * 3,
        scratch_shapes=[
            pltpu.VMEM(flat, F32),
            pltpu.VMEM(flat, F32),
            pltpu.VMEM(conductivity.shape, F32),
            pltpu.VMEM(fsai_diagonal.shape, F32),
            pltpu.VMEM(fsai_lower.shape, F32),
            pltpu.SMEM(pattern.shape, jnp.int32),
            pltpu.SMEM(step_size.shape, F32),
            pltpu.SMEM(momentum.shape, F32),
            padded(1, 1), padded(1, 1), padded(1, 2), padded(1, 1), padded(1, 1), padded(1, 1),
            pltpu.VMEM((size_y,) + column, F32),
            pltpu.VMEM((size_x,) + column, F32),
            pltpu.VMEM((size_x,) + column, F32),
            pltpu.VMEM((2,) + column, F32),
            pltpu.VMEM((size_y,) + column, F32),
            pltpu.VMEM((size_x,) + column, F32),
            pltpu.VMEM((size_x,) + column, F32),
            pltpu.VMEM((2,) + column, F32),
            pltpu.VMEM((size_y,) + column, F32),
            pltpu.VMEM((size_x,) + column, F32),
            pltpu.VMEM((4, size_y, size_z), F32),
            pltpu.VMEM((2, size_x, size_z), F32),
            pltpu.VMEM((7, size_x, size_y, size_z), F32),
            pltpu.VMEM((terms, size_x + 2, size_y + 8, size_z), F32),
            pltpu.VMEM((terms - 1, size_x, size_y, size_z), F32),
            pltpu.VMEM((6 * vectors, cells * size_z), BF16),
            pltpu.VMEM((6 * vectors, (size_x + size_y) * size_z), BF16),
            pltpu.VMEM((nx,) + column, F32),
            pltpu.VMEM((ny,) + column, F32),
            pltpu.VMEM((nx,) + column, F32),
            pltpu.VMEM((ny,) + column, F32),
            pltpu.VMEM((nx,) + column, F32),
            pltpu.VMEM((ny,) + column, F32),
            pltpu.SemaphoreType.DMA((8,)),
            pltpu.SemaphoreType.DMA((27,)),
            pltpu.SemaphoreType.DMA((27,)),
            pltpu.SemaphoreType.DMA((3, nx)),
            pltpu.SemaphoreType.DMA((3, nx)),
            pltpu.SemaphoreType.DMA((3, ny)),
            pltpu.SemaphoreType.DMA((3, ny)),
        ],
        compiler_params=pltpu.CompilerParams(
            collective_id=0, has_side_effects=True, vmem_limit_bytes=62 * 1024 * 1024
        ),
    )(
        x_block.reshape(flat), old_direction.reshape(flat), conductivity, fsai_diagonal,
        fsai_lower, pattern, step_size, momentum,
    )
    return x_next.reshape(x_block.shape), direction.reshape(x_block.shape), rayleigh


def solution(mesh):
    placed = (
        P(None, "gx", "gy", None),
        P(None, "gx", "gy", None),
        P("gx", "gy", None),
        P("gx", "gy", None),
        P(None, "gx", "gy", None),
        P(),
        P(),
        P(),
    )
    return jax.shard_map(
        per_device,
        mesh=mesh,
        in_specs=placed,
        out_specs=(P(None, "gx", "gy", None), P(None, "gx", "gy", None), P()),
        check_vma=False,
    )
```

```python
import functools

import jax
import jax.numpy as jnp
from jax import lax
from jax.experimental import pallas as pl
from jax.experimental.pallas import tpu as pltpu
from jax.sharding import PartitionSpec as P

MESH = pl.DeviceIdType.MESH
F32 = jnp.float32
BF16 = jnp.bfloat16

lower_offsets = [
    (a, b, c) for a in (-1, 0, 1) for b in (-1, 0, 1) for c in (-1, 0, 1) if (a, b, c) < (0, 0, 0)
]
DIAG = len(lower_offsets)
SIDES = [(1, 0), (-1, 0), (0, 1), (0, -1)]


def split3(value):
    high = value.astype(BF16)
    rest = value - high.astype(F32)
    middle = rest.astype(BF16)
    low = (rest - middle.astype(F32)).astype(BF16)
    return high, middle, low


def kernel(
    nx, ny, scale,
    x_hbm, old_hbm, cond_hbm, diag_hbm, lower_hbm, pattern_hbm, step_hbm, mom_hbm,
    next_hbm, dir_hbm, ray_out,
    x_in, old_in, cond_in, diag_in, lower_in, pattern_in, step_in, mom_in,
    xs, im, pr, ptx, pt, adv,
    rx_x, rx_y0, rx_y1, rx_c, recv_x, recv_y0, recv_y1, recv_c, halo_x, halo_y,
    k_side, k_stage, coef, lm, lp,
    ab, abh, q_x, q_y, g_x, g_y, s_x, s_y,
    next_out, dir_out, store_sem,
    load_sem, send_sem, recv_sem, send_x, recv_gx, send_y, recv_gy,
):
    loads = [
        pltpu.make_async_copy(src, dst, load_sem.at[i])
        for i, (src, dst) in enumerate((
            (x_hbm, x_in), (cond_hbm, cond_in), (pattern_hbm, pattern_in), (lower_hbm, lower_in),
            (diag_hbm, diag_in), (step_hbm, step_in), (mom_hbm, mom_in), (old_hbm, old_in),
        ))
    ]
    for load in loads:
        load.start()
    ix, iy = lax.axis_index("gx"), lax.axis_index("gy")
    size_x, size_y = cond_in.shape[0], cond_in.shape[1]
    depth = cond_in.shape[2]
    vectors = xs.shape[2]
    cells = size_x * size_y
    blocks = pattern_in.shape[0]
    zero_col = jnp.zeros((vectors, depth), F32)
    zero_tile = jnp.zeros((size_y, depth), F32)

    def exists(sx, sy):
        found = None
        for ok, step in (
            (ix + 1 < nx, sx > 0), (ix > 0, sx < 0), (iy + 1 < ny, sy > 0), (iy > 0, sy < 0)
        ):
            if step:
                found = ok if found is None else jnp.logical_and(found, ok)
        return found

    def copy_of(item):
        src, dst, sx, sy, slot = item
        return pltpu.make_async_remote_copy(
            src_ref=src, dst_ref=dst, send_sem=send_sem.at[slot], recv_sem=recv_sem.at[slot],
            device_id=(ix + sx, iy + sy), device_id_type=MESH,
        )

    def start(items):
        for item in items:
            @pl.when(exists(item[2], item[3]))
            def _(item=item):
                copy_of(item).start()

    def wait_recv(items):
        for item in items:
            @pl.when(exists(-item[2], -item[3]))
            def _(item=item):
                copy_of(item).wait_recv()

    def wait_send(items):
        for item in items:
            @pl.when(exists(item[2], item[3]))
            def _(item=item):
                copy_of(item).wait_send()

    def group_start(buf, turn, n, me, place, sends, recvs):
        for s in range(1, n):
            peer = lax.rem(me + s, n)
            pltpu.make_async_remote_copy(
                src_ref=buf.at[me], dst_ref=buf.at[me], send_sem=sends.at[turn, s],
                recv_sem=recvs.at[turn, s], device_id=place(peer), device_id_type=MESH,
            ).start()

    def group_wait(buf, turn, n, me, place, sends, recvs):
        for s in range(1, n):
            peer = lax.rem(me + n - s, n)
            pltpu.make_async_remote_copy(
                src_ref=buf.at[peer], dst_ref=buf.at[peer], send_sem=sends.at[turn, s],
                recv_sem=recvs.at[turn, s], device_id=place(peer), device_id_type=MESH,
            ).wait()

    def along_x(peer):
        return (peer, iy)

    def along_y(peer):
        return (ix, peer)

    def reduce_start(buf_x, turn, tile):
        buf_x[ix] = tile
        group_start(buf_x, turn, nx, ix, along_x, send_x, recv_gx)

    def reduce_middle(buf_x, buf_y, turn):
        group_wait(buf_x, turn, nx, ix, along_x, send_x, recv_gx)
        total = buf_x[0]
        for i in range(1, nx):
            total = total + buf_x[i]
        buf_y[iy] = total
        group_start(buf_y, turn, ny, iy, along_y, send_y, recv_gy)

    def reduce_finish(buf_y, turn):
        group_wait(buf_y, turn, ny, iy, along_y, send_y, recv_gy)
        total = buf_y[0]
        for i in range(1, ny):
            total = total + buf_y[i]
        return total

    for buf in (xs, im):
        for y in range(size_y + 2):
            buf[0, y] = zero_col
            buf[size_x + 1, y] = zero_col
        for x in range(1, size_x + 1):
            buf[x, 0] = zero_col
            buf[x, size_y + 1] = zero_col
    for i in range(4):
        k_side[i] = zero_tile
    for buf in (rx_x, rx_y0, rx_y1, rx_c, recv_x, recv_y0, recv_y1, recv_c, halo_x, halo_y):
        for i in range(buf.shape[0]):
            buf[i] = zero_col

    barrier = pltpu.get_barrier_semaphore()
    for s in range(1, nx):
        pl.semaphore_signal(barrier, inc=1, device_id=along_x(lax.rem(ix + s, nx)), device_id_type=MESH)
    for s in range(1, ny):
        pl.semaphore_signal(barrier, inc=1, device_id=along_y(lax.rem(iy + s, ny)), device_id_type=MESH)
    diagonal = 0
    for sx in (-1, 1):
        for sy in (-1, 1):
            there = exists(sx, sy)
            diagonal = diagonal + jnp.where(there, 1, 0)

            @pl.when(there)
            def _(sx=sx, sy=sy):
                pl.semaphore_signal(barrier, inc=1, device_id=(ix + sx, iy + sy), device_id_type=MESH)

    loads[0].wait()
    loads[1].wait()

    def turn_in(x, _):
        for y in range(size_y):
            xs[x + 1, y + 1] = x_in[pl.ds(x * size_y + y, vectors, stride=cells), :]
        return 0

    lax.fori_loop(0, size_x, turn_in, 0)
    k_stage[0] = cond_in[:, size_y - 1, :]
    k_stage[1] = cond_in[:, 0, :]

    pl.semaphore_wait(barrier, nx - 1 + ny - 1 + diagonal)

    inner_x, inner_y = pl.ds(1, size_x), pl.ds(1, size_y)
    first = [
        (k_stage.at[0], k_side.at[2], 0, 1, 0),
        (k_stage.at[1], k_side.at[3], 0, -1, 1),
        (cond_in.at[size_x - 1], k_side.at[0], 1, 0, 2),
        (cond_in.at[0], k_side.at[1], -1, 0, 3),
        (xs.at[inner_x, size_y], xs.at[inner_x, 0], 0, 1, 4),
        (xs.at[inner_x, 1], xs.at[inner_x, size_y + 1], 0, -1, 5),
        (xs.at[size_x, inner_y], xs.at[0, inner_y], 1, 0, 6),
        (xs.at[1, inner_y], xs.at[size_x + 1, inner_y], -1, 0, 7),
        (xs.at[size_x, size_y], xs.at[0, 0], 1, 1, 8),
        (xs.at[size_x, 1], xs.at[0, size_y + 1], 1, -1, 9),
    ]
    start(first)

    for load in loads[2:]:
        load.wait()
    lane = lax.broadcasted_iota(jnp.int32, (size_y, depth), 1)
    piece = lane // (depth // blocks)
    for o in range(DIAG):
        dz = lower_offsets[o][2]
        keep = jnp.zeros((size_y, depth), F32)
        for b in range(blocks):
            keep = jnp.where(piece == b, pattern_in[b, o].astype(F32), keep)
        if dz:
            keep = jnp.where(lane == (0 if dz < 0 else depth - 1), 0.0, keep)

        for x in range(size_x):
            term = lower_in[o, x] * keep
            lm[o, x + 1, pl.ds(2, size_y), :] = term
            lp[o, x] = pltpu.roll(term, dz % depth, 1) if dz else term

    for x in range(size_x):
        lm[DIAG, x + 1, pl.ds(2, size_y), :] = diag_in[x]

    def rims(o, _):
        for x in range(size_x + 2):
            if x in (0, size_x + 1):
                lm[o, x] = jnp.zeros((lm.shape[2], depth), F32)
            else:
                lm[o, x, pl.ds(0, 2), :] = jnp.zeros((2, depth), F32)
                lm[o, x, pl.ds(size_y + 2, 2), :] = jnp.zeros((2, depth), F32)
        return 0

    lax.fori_loop(0, DIAG + 1, rims, 0)
    for y in range(size_y + 4):
        pr[0, y] = zero_col
        pr[size_x + 1, y] = zero_col
    for x in range(1, size_x + 1):
        for y in (0, 1, size_y + 2, size_y + 3):
            pr[x, y] = zero_col
    for y in range(size_y + 2):
        adv[0, y] = zero_col
        adv[size_x + 1, y] = zero_col
    for x in range(1, size_x + 1):
        adv[x, 0] = zero_col
        adv[x, size_y + 1] = zero_col

    row = lax.broadcasted_iota(jnp.int32, (vectors, depth), 0)
    step_col, mom_col = zero_col, zero_col
    for k in range(vectors):
        step_col = jnp.where(row == k, step_in[k], step_col)
        mom_col = jnp.where(row == k, mom_in[k], mom_col)

    wait_recv(first[:4])
    row8 = lax.broadcasted_iota(jnp.int32, (size_y, depth), 0)

    for x in range(size_x):
        here = cond_in[x]
        below = k_side[0] if x == 0 else cond_in[x - 1]
        above = k_side[1] if x == size_x - 1 else cond_in[x + 1]
        left = jnp.where(row8 == 0, k_side[2, pl.ds(x, 1), :], pltpu.roll(here, 1, 0))
        right = jnp.where(row8 == size_y - 1, k_side[3, pl.ds(x, 1), :], pltpu.roll(here, size_y - 1, 0))
        back = jnp.where(lane == 0, 0.0, pltpu.roll(here, 1, 1))
        front = jnp.where(lane == depth - 1, 0.0, pltpu.roll(here, depth - 1, 1))
        total = None
        for i, near in enumerate((below, above, left, right, back, front)):
            face = 0.5 * (here + near)
            total = face if total is None else total + face
            if i == 4:
                face = jnp.where(lane == 0, 0.0, face)
            if i == 5:
                face = jnp.where(lane == depth - 1, 0.0, face)
            coef[i + 1, x] = face
        coef[0, x] = total

    def stiffness(buf, x, y):
        centre = buf[x + 1, y + 1]

        def c(i):
            return coef[i, x, pl.ds(y, 1), :]

        return (
            c(0) * centre
            - c(1) * buf[x, y + 1] - c(2) * buf[x + 2, y + 1]
            - c(3) * buf[x + 1, y] - c(4) * buf[x + 1, y + 2]
            - c(5) * pltpu.roll(centre, 1, 1) - c(6) * pltpu.roll(centre, depth - 1, 1)
        )

    def image_at(x, y, sums):
        centre = xs[x + 1, y + 1]
        image = stiffness(xs, x, y)
        im[x + 1, y + 1] = image
        return sums[0] + centre * centre, sums[1] + centre * image

    def inner_images(x, sums):
        for y in range(1, size_y - 1):
            sums = image_at(x, y, sums)
        return sums

    def side_images(x, sums):
        return image_at(x, size_y - 1, image_at(x, 0, sums))

    sums = lax.fori_loop(1, size_x - 1, inner_images, (zero_col, zero_col))
    wait_recv(first[4:])
    sums = lax.fori_loop(0, size_x, side_images, sums)
    sums = inner_images(size_x - 1, inner_images(0, sums))
    second = [
        (im.at[inner_x, size_y], im.at[inner_x, 0], 0, 1, 10),
        (im.at[inner_x, 1], im.at[inner_x, size_y + 1], 0, -1, 11),
        (im.at[size_x, inner_y], im.at[0, inner_y], 1, 0, 12),
        (im.at[size_x, size_y], im.at[0, 0], 1, 1, 13),
        (im.at[size_x, 1], im.at[0, size_y + 1], 1, -1, 14),
    ]
    start(second)
    sum_xx, sum_xa = sums
    lane16 = lax.broadcasted_iota(jnp.int32, (vectors, depth), 1)
    both = jnp.where(
        lane16 < depth // 2,
        jnp.sum(sum_xx, axis=1, keepdims=True), jnp.sum(sum_xa, axis=1, keepdims=True),
    )
    reduce_start(q_x, 0, both)

    def factor(buf):
        def products(x, _):
            for y in range(size_y):
                parts = {0: diag_in[x, pl.ds(y, 1), :] * buf[x + 1, y + 1], -1: zero_col, 1: zero_col}
                for o, (dx, dy, dz) in enumerate(lower_offsets):
                    parts[dz] = parts[dz] + lp[o, x, pl.ds(y, 1), :] * buf[x + 1 + dx, y + 1 + dy]
                pr[x + 1, y + 2] = (
                    parts[0] + pltpu.roll(parts[-1], 1, 1) + pltpu.roll(parts[1], depth - 1, 1)
                )
            return 0

        lax.fori_loop(0, size_x, products, 0)

    def transposed(out, arrivals, slot):
        def target(x, y):
            parts = {0: lm[DIAG, x, pl.ds(y + 1, 1), :] * pr[x, y + 1], -1: zero_col, 1: zero_col}
            for o, (dx, dy, dz) in enumerate(lower_offsets):
                parts[dz] = parts[dz] + lm[o, x - dx, pl.ds(y + 1 - dy, 1), :] * pr[x - dx, y + 1 - dy]
            out[x, y] = parts[0] + pltpu.roll(parts[-1], depth - 1, 1) + pltpu.roll(parts[1], 1, 1)

        for y in range(size_y + 2):
            target(0, y)

        def rim_targets(x, _):
            target(x, 0)
            target(x, size_y + 1)
            return 0

        lax.fori_loop(1, size_x + 1, rim_targets, 0)
        to_x, to_y0, to_y1, to_c = arrivals
        items = [
            (out.at[inner_x, 0], to_y0, 0, -1, slot),
            (out.at[inner_x, size_y + 1], to_y1, 0, 1, slot + 1),
            (out.at[0, inner_y], to_x, -1, 0, slot + 2),
            (out.at[0, 0], to_c.at[0], -1, -1, slot + 3),
            (out.at[0, size_y + 1], to_c.at[1], -1, 1, slot + 4),
        ]
        start(items)

        def own_targets(x, _):
            for y in range(1, size_y + 1):
                target(x, y)
            return 0

        lax.fori_loop(1, size_x + 1, own_targets, 0)
        return items

    def gather(out, arrivals, items):
        wait_recv(items)
        to_x, to_y0, to_y1, to_c = arrivals
        for y in range(size_y):
            out[size_x, y + 1] = out[size_x, y + 1] + to_x[y]
        for x in range(size_x):
            out[x + 1, size_y] = out[x + 1, size_y] + to_y0[x]
            out[x + 1, 1] = out[x + 1, 1] + to_y1[x]
        out[size_x, size_y] = out[size_x, size_y] + to_c[0]
        out[size_x, 1] = out[size_x, 1] + to_c[1]

    arrivals_x = (rx_x, rx_y0, rx_y1, rx_c)
    arrivals = (recv_x, recv_y0, recv_y1, recv_c)
    factor(xs)
    third_x = transposed(ptx, arrivals_x, 22)
    reduce_middle(q_x, q_y, 0)
    wait_recv(second)
    factor(im)
    third = transposed(pt, arrivals, 15)
    gather(ptx, arrivals_x, third_x)
    both = reduce_finish(q_y, 0)
    quotient = both[:, depth // 2 : depth // 2 + 1] * scale / (both[:, 0:1] * scale + 1e-06)
    quotient = jnp.broadcast_to(quotient, (vectors, depth))
    gather(pt, arrivals, third)

    def at_column(index):
        return pl.ds(pl.multiple_of(index * depth, depth), depth)

    def put(buf, base, index, value):
        for i, part in enumerate(split3(value)):
            buf[base + i * vectors : base + (i + 1) * vectors, at_column(index)] = part

    def advance(x, _):
        for y in range(size_y):
            spot = pl.ds(x * size_y + y, vectors, stride=cells)
            direction = (pt[x + 1, y + 1] - quotient * ptx[x + 1, y + 1]) + mom_col * old_in[spot, :]
            dir_out[spot, :] = direction
            advanced = xs[x + 1, y + 1] + step_col * direction
            adv[x + 1, y + 1] = advanced
            put(ab, 0, x * size_y + y, advanced)
        return 0

    lax.fori_loop(0, size_x, advance, 0)
    fourth = [
        (adv.at[inner_x, 1], halo_y, 0, -1, 20),
        (adv.at[1, inner_y], halo_x, -1, 0, 21),
    ]
    start(fourth)
    dir_store = pltpu.make_async_copy(dir_out, dir_hbm, store_sem.at[0])
    dir_store.start()
    nt = (((1,), (1,)), ((), ()))
    third_rows = 3 * vectors

    def collect(array):
        return sum(
            array[i * vectors : (i + 1) * vectors, j * vectors : (j + 1) * vectors]
            for i in range(3) for j in range(3)
        )

    half_rows = vectors // 2

    def as_tile(array):
        empty = jnp.zeros((half_rows, depth - 2 * vectors), F32)
        return jnp.concatenate([array[:half_rows], array[half_rows:], empty], axis=1)

    def from_tile(tile):
        return jnp.concatenate([tile, pltpu.roll(tile, depth - vectors, 1)], axis=0)

    gram = collect(lax.dot_general(
        ab[0:third_rows, :], ab[0:third_rows, :], nt, preferred_element_type=F32
    ))
    reduce_start(g_x, 1, as_tile(gram))

    def advanced_images(x, _):
        for y in range(size_y):
            put(ab, third_rows, x * size_y + y, stiffness(adv, x, y))
        return 0

    lax.fori_loop(0, size_x, advanced_images, 0)
    reduce_middle(g_x, g_y, 1)
    stiff = collect(lax.dot_general(
        ab[0:third_rows, :], ab[third_rows:, :], nt, preferred_element_type=F32
    ))
    wait_recv(fourth)
    for y in range(size_y):
        put(abh, 0, y, adv[size_x, y + 1])
        put(abh, third_rows, y, -coef[2, size_x - 1, pl.ds(y, 1), :] * halo_x[y])
    for x in range(size_x):
        put(abh, 0, size_y + x, adv[x + 1, size_y])
        put(abh, third_rows, size_y + x, -coef[4, x, pl.ds(size_y - 1, 1), :] * halo_y[x])
    crossed = lax.dot_general(abh[...], abh[...], nt, preferred_element_type=F32)
    stiff = stiff + collect(crossed[0:third_rows, third_rows:]) + collect(crossed[third_rows:, 0:third_rows])
    reduce_start(s_x, 2, as_tile(stiff))

    total = jnp.where(lane16 < vectors, from_tile(reduce_finish(g_y, 1)), 0.0)
    aug = total * scale + jnp.where(row == lane16, 1e-05, 0.0)
    aug = aug + jnp.where(row + vectors == lane16, 1.0, 0.0)
    for j in range(vectors - 1):
        ratio = aug[:, j : j + 1] / aug[j : j + 1, j : j + 1]
        aug = aug - jnp.where(row > j, ratio * aug[j : j + 1, :], 0.0)
    pivots = jnp.sum(jnp.where(row == lane16, aug, 0.0), axis=1, keepdims=True)
    aug = aug / jnp.sqrt(pivots)
    inverse = aug[:, vectors : 2 * vectors]
    reduce_middle(s_x, s_y, 2)
    weights = jnp.concatenate(
        [jnp.concatenate([part.astype(F32)] * 3, axis=1) for part in split3(inverse)], axis=0
    ).astype(BF16)

    def rows(array):
        return array[:vectors] + array[vectors : 2 * vectors] + array[2 * vectors :]

    def rotate(x, _):
        wide_part = pl.ds(pl.multiple_of(x * size_y * depth, depth), size_y * depth)
        mixed = rows(
            jnp.dot(weights, ab[0 : 3 * vectors, wide_part], preferred_element_type=F32)
        )
        for y in range(size_y):
            next_out[pl.ds(x * size_y + y, vectors, stride=cells), :] = mixed[
                :, y * depth : (y + 1) * depth
            ]
        return 0

    lax.fori_loop(0, size_x, rotate, 0)
    next_store = pltpu.make_async_copy(next_out, next_hbm, store_sem.at[1])
    next_store.start()
    stiff = (from_tile(reduce_finish(s_y, 2)) * scale)[:, 0:vectors]
    highest = lax.Precision.HIGHEST
    half = jnp.dot(inverse, stiff, preferred_element_type=F32, precision=highest)
    ray_out[...] = lax.dot_general(half, inverse, nt, preferred_element_type=F32, precision=highest)
    for items in (first, second, third_x, third, fourth):
        wait_send(items)
    dir_store.wait()
    next_store.wait()


def per_device(
    x_block, old_direction, conductivity, fsai_diagonal, fsai_lower, pattern, step_size, momentum
):
    vectors, size_x, size_y, size_z = x_block.shape
    nx, ny = lax.axis_size("gx"), lax.axis_size("gy")
    cells = size_x * size_y
    scale = 1.0 / (cells * size_z * nx * ny)
    flat = (vectors * cells, size_z)
    column = (vectors, size_z)
    vmem = pl.BlockSpec(memory_space=pltpu.VMEM)
    hbm = pl.BlockSpec(memory_space=pltpu.HBM)

    def padded(rx, ry):
        return pltpu.VMEM((size_x + 2 * rx, size_y + 2 * ry) + column, F32)

    terms = fsai_lower.shape[0] + 1
    x_next, direction, rayleigh = pl.pallas_call(
        functools.partial(kernel, nx, ny, scale),
        out_shape=[
            jax.ShapeDtypeStruct(flat, F32),
            jax.ShapeDtypeStruct(flat, F32),
            jax.ShapeDtypeStruct((vectors, vectors), F32),
        ],
        in_specs=[hbm] * 8,
        out_specs=[hbm, hbm, vmem],
        scratch_shapes=[
            pltpu.VMEM(flat, F32),
            pltpu.VMEM(flat, F32),
            pltpu.VMEM(conductivity.shape, F32),
            pltpu.VMEM(fsai_diagonal.shape, F32),
            pltpu.VMEM(fsai_lower.shape, F32),
            pltpu.SMEM(pattern.shape, jnp.int32),
            pltpu.SMEM(step_size.shape, F32),
            pltpu.SMEM(momentum.shape, F32),
            padded(1, 1), padded(1, 1), padded(1, 2), padded(1, 1), padded(1, 1), padded(1, 1),
            pltpu.VMEM((size_y,) + column, F32),
            pltpu.VMEM((size_x,) + column, F32),
            pltpu.VMEM((size_x,) + column, F32),
            pltpu.VMEM((2,) + column, F32),
            pltpu.VMEM((size_y,) + column, F32),
            pltpu.VMEM((size_x,) + column, F32),
            pltpu.VMEM((size_x,) + column, F32),
            pltpu.VMEM((2,) + column, F32),
            pltpu.VMEM((size_y,) + column, F32),
            pltpu.VMEM((size_x,) + column, F32),
            pltpu.VMEM((4, size_y, size_z), F32),
            pltpu.VMEM((2, size_x, size_z), F32),
            pltpu.VMEM((7, size_x, size_y, size_z), F32),
            pltpu.VMEM((terms, size_x + 2, size_y + 8, size_z), F32),
            pltpu.VMEM((terms - 1, size_x, size_y, size_z), F32),
            pltpu.VMEM((6 * vectors, cells * size_z), BF16),
            pltpu.VMEM((6 * vectors, (size_x + size_y) * size_z), BF16),
            pltpu.VMEM((nx,) + column, F32),
            pltpu.VMEM((ny,) + column, F32),
            pltpu.VMEM((nx, vectors // 2, size_z), F32),
            pltpu.VMEM((ny, vectors // 2, size_z), F32),
            pltpu.VMEM((nx, vectors // 2, size_z), F32),
            pltpu.VMEM((ny, vectors // 2, size_z), F32),
            pltpu.VMEM(flat, F32),
            pltpu.VMEM(flat, F32),
            pltpu.SemaphoreType.DMA((2,)),
            pltpu.SemaphoreType.DMA((8,)),
            pltpu.SemaphoreType.DMA((27,)),
            pltpu.SemaphoreType.DMA((27,)),
            pltpu.SemaphoreType.DMA((3, nx)),
            pltpu.SemaphoreType.DMA((3, nx)),
            pltpu.SemaphoreType.DMA((3, ny)),
            pltpu.SemaphoreType.DMA((3, ny)),
        ],
        compiler_params=pltpu.CompilerParams(
            collective_id=0, has_side_effects=True, vmem_limit_bytes=62 * 1024 * 1024
        ),
    )(
        x_block.reshape(flat), old_direction.reshape(flat), conductivity, fsai_diagonal,
        fsai_lower, pattern, step_size, momentum,
    )
    return x_next.reshape(x_block.shape), direction.reshape(x_block.shape), rayleigh


def solution(mesh):
    placed = (
        P(None, "gx", "gy", None),
        P(None, "gx", "gy", None),
        P("gx", "gy", None),
        P("gx", "gy", None),
        P(None, "gx", "gy", None),
        P(),
        P(),
        P(),
    )
    return jax.shard_map(
        per_device,
        mesh=mesh,
        in_specs=placed,
        out_specs=(P(None, "gx", "gy", None), P(None, "gx", "gy", None), P()),
        check_vma=False,
    )
```
